32 devices in a mesh: slab: 2 (over y), col: 4 (over z), row: 2 (over x), ch: 2 (over core).
Axes of the slice: x: 2, y: 2, z: 4, core: 2. Of those that a mesh axis runs over, the one named last changes fastest.
Arguments:
- left_feat: bfloat16 [128, 128, 1024], P(('slab', 'row'), 'ch', 'col'), parts along dimension 0, may hold values from -512 to 512
- right_feat: bfloat16 [128, 128, 1024], P(('slab', 'row'), 'ch', 'col'), parts along dimension 0, may hold values from -12 to 12
- offsets: int32 [8], P(('slab', 'col')), parts along dimension 0, may hold values from 0 to 256, as said below
- valid: int32 [128, 1024], P(('slab', 'row'), ('col', 'ch')), parts along dimension 0, may hold values 0 or 1
- w_first: float32 [3, 3, 32, 2], replicated, may hold values from -1.5 to 1.5
- w_middle: float32 [3, 3, 32, 32], replicated, may hold values from -0.375 to 0.375
- w_last: float32 [3, 3, 1, 32], replicated, may hold values from -0.375 to 0.375
- grad_out: float32 [128, 1024], P(('slab', 'row'), ('col', 'ch')), parts along dimension 0, may hold values from -6 to 6
Outputs:
- refined: float32 [128, 1024], P(('slab', 'row'), ('col', 'ch')), parts along dimension 0
- grad_left: bfloat16 [128, 128, 1024], P(('slab', 'row'), 'ch', 'col'), parts along dimension 0
- grad_right: bfloat16 [128, 128, 1024], P(('slab', 'row'), 'ch', 'col'), parts along dimension 0
The draws below stay inside these ranges and needn't reach their ends.
There are 2 independent parts, one for each index of `slab`. The reference program is written for one: setup_inputs(seed, part) draws one part's arguments, and reference() takes and returns one part's arrays. A program takes and returns all parts, laid end to end along the dimension named above; an argument that names none is the same for every part. Nothing has to cross between parts.
Inputs may be any that keep to these rules, and one draw needn't show every extreme that they name: `offsets`: the largest tile offset is exactly 256 in every draw.
All inputs are finite; a program needn't handle non-finite values. No bound on the sum of `valid` on one device may be relied on, other than what follows from the above.
Results may differ from the reference program's by a relative error of at most 0.005.
Values may be sent and summed in bfloat16 or wider, within the bound.
A program may use at most 128 MiB of HBM per device.

```python
import math
import jax
import jax.numpy as jnp
from jax import lax

FEAT = 128
DISP = 256
REFINE = 32
W_DEV = 256
H = 64
COL_TILES = 4
W = 1024
OFFMAX = 256


def band_offsets(key):
    base_key = jax.random.fold_in(key, 11)
    values = jax.random.randint(base_key, (COL_TILES,), 0, OFFMAX + 1, dtype=jnp.int32)
    chosen = jax.random.randint(jax.random.fold_in(base_key, 1), (), 0, COL_TILES, dtype=jnp.int32)
    return jnp.where(jnp.arange(COL_TILES, dtype=jnp.int32) == chosen, OFFMAX, values).astype(jnp.int32)


def feature_pair(key):
    right_vals = jax.random.normal(jax.random.fold_in(key, 21), (H, W, FEAT), jnp.float32)
    left_vals = jax.random.normal(jax.random.fold_in(key, 22), (H, W, FEAT), jnp.float32)
    left_out = jnp.transpose(jnp.clip(left_vals, -512.0, 512.0), (0, 2, 1))
    right_out = jnp.transpose(jnp.clip(right_vals, -12.0, 12.0), (0, 2, 1))
    return (left_out, right_out)


def draw_left_feat(key, part):
    return feature_pair(key)[0].astype(jnp.bfloat16)


def draw_right_feat(key, part):
    return feature_pair(key)[1].astype(jnp.bfloat16)


def draw_offsets(key, part):
    return band_offsets(key)


def with_ends(entries, rng, low, top_value):
    index_at = [jax.random.randint(jax.random.fold_in(rng, axis), (), 0, length) for axis, length in enumerate(entries.shape)]
    main_axis = entries.shape.index(max(entries.shape))
    beside = index_at[:main_axis] + [(index_at[main_axis] + 1) % entries.shape[main_axis]] + index_at[main_axis + 1:]
    return entries.at[tuple(index_at)].set(low).at[tuple(beside)].set(top_value)


def block_levels(key, dims, split, low, top_value):
    loudness = 1.0
    for dim, shards_of in split:
        draws = jax.random.uniform(jax.random.fold_in(jax.random.fold_in(key, 6), dim), (shards_of,), jnp.float32, low / len(split), top_value / len(split))
        loudness = loudness * jnp.repeat(jnp.exp(draws), dims[dim] // shards_of).reshape((-1,) + (1,) * (len(dims) - 1 - dim))
    return loudness


def scatter_about(stream_key, shape, deviation, most, cuts=(), kind=jnp.bfloat16):
    loudness = block_levels(stream_key, shape, cuts, -0.22, 0.18) if cuts else 1.0
    array = jax.random.normal(stream_key, shape, jnp.float32) * deviation * loudness
    return jnp.minimum(jnp.maximum(array, -most), most).astype(kind)


def setup_inputs(seed: int = 0, part: int = 0) -> dict:
    streams_of = jax.random.split(jax.random.key(seed), 9)
    part_keys = jax.random.split(jax.random.fold_in(streams_of[8], part), 9)
    return {
        "left_feat": draw_left_feat(jax.random.fold_in(jax.random.fold_in(streams_of[8], part), 71), part),
        "right_feat": draw_right_feat(jax.random.fold_in(jax.random.fold_in(streams_of[8], part), 71), part),
        "offsets": draw_offsets(jax.random.fold_in(jax.random.fold_in(streams_of[8], part), 71), part),
        "valid": with_ends((jax.random.randint(part_keys[3], (H, W), 0, 8) < 7).astype(jnp.int32), jax.random.fold_in(part_keys[3], 1), 0, 1),
        "w_first": scatter_about(streams_of[4], (3, 3, REFINE, 2), 18 ** -0.5, 1.5, (), jnp.float32),
        "w_middle": scatter_about(streams_of[5], (3, 3, REFINE, REFINE), (9 * REFINE) ** -0.5, 0.375, (), jnp.float32),
        "w_last": scatter_about(streams_of[6], (3, 3, 1, REFINE), (9 * REFINE) ** -0.5, 0.375, (), jnp.float32),
        "grad_out": scatter_about(part_keys[7], (H, W), 1.0, 6.0, ((0, 2), (1, 8)), jnp.float32),
    }


def skew_out(products):
    tile_rows, band_span = products.shape
    flat_rows = jnp.concatenate([products.reshape(-1), jnp.zeros((tile_rows,), products.dtype)])
    return flat_rows.reshape(tile_rows, band_span + 1)[:, 1:DISP + 1]

def skew_in(band_vals, band_span):
    tile_rows = band_vals.shape[0]
    padded = jnp.pad(band_vals, ((0, 0), (1, band_span - DISP)))
    return padded.reshape(-1)[:tile_rows * band_span].reshape(tile_rows, band_span)

def band_stats(scores, offset_term):
    probs = jax.nn.softmax(scores, axis=-1)
    levels = (DISP - 1 - jnp.arange(DISP).astype(jnp.float32)) / DISP
    mean_level = lax.optimization_barrier(jnp.sum(probs * levels, axis=-1))
    coarse = offset_term / DISP + mean_level
    spread = lax.optimization_barrier(jnp.sum(probs * (levels - mean_level[..., None]) ** 2, axis=-1))
    return (coarse, spread)

def conv_taps(padded, weights, rows_out, cols_out):
    result = jnp.zeros((weights.shape[2], rows_out, cols_out), jnp.float32)
    for tap_row in range(3):
        for tap_col in range(3):
            result = result + jnp.einsum('oi,ihw->ohw', weights[tap_row, tap_col], padded[:, tap_row:tap_row + rows_out, tap_col:tap_col + cols_out], precision=lax.Precision.HIGHEST)
    return result

def conv_same(field, weights):
    padded = jnp.pad(field, ((0, 0), (1, 1), (1, 1)))
    return conv_taps(padded, weights, field.shape[1], field.shape[2])

def refine(coarse, spread, valid_f, w_first, w_middle, w_last):
    inputs = jnp.stack([coarse * valid_f, spread * valid_f])
    hidden_one = jax.nn.silu(conv_same(inputs, w_first))
    hidden_two = jax.nn.silu(conv_same(hidden_one, w_middle))
    return valid_f * (coarse + conv_same(hidden_two, w_last)[0])

def reference(left_feat, right_feat, offsets, valid, w_first, w_middle, w_last, grad_out):
    left_feat = jnp.transpose(left_feat, (0, 2, 1))
    right_feat = jnp.transpose(right_feat, (0, 2, 1))
    pad_left = OFFMAX + DISP
    band_span = W_DEV + DISP
    right_pad = jnp.pad(right_feat, ((0, 0), (pad_left, 0), (0, 0)))
    tile_ids = jnp.arange(COL_TILES).astype(jnp.int32)
    row_ids = jnp.arange(H).astype(jnp.int32)

    def tile_inputs(row_index, tile_index):
        left_row = lax.dynamic_index_in_dim(left_feat, row_index, 0, keepdims=False)
        right_row = lax.dynamic_index_in_dim(right_pad, row_index, 0, keepdims=False)
        left_tile = lax.dynamic_slice_in_dim(left_row, (tile_index * W_DEV).astype(jnp.int32), W_DEV, 0)
        start_col = (tile_index * W_DEV - offsets[tile_index] - DISP + pad_left).astype(jnp.int32)
        right_band = lax.dynamic_slice_in_dim(right_row, start_col, band_span, 0)
        return (left_tile, right_band, start_col)

    def cost_row(row_index):

        def cost_tile(tile_index):
            left_tile, right_band, start_col = tile_inputs(row_index, tile_index)
            products = jnp.dot(left_tile, right_band.T, preferred_element_type=jnp.float32)
            return skew_out(products)
        return lax.map(cost_tile, tile_ids).reshape(W, DISP)
    cost = lax.map(cost_row, row_ids)
    offset_cols = jnp.repeat(offsets, W_DEV).astype(jnp.float32)
    valid_f = valid.astype(jnp.float32)
    (coarse, spread), stats_back = jax.vjp(lambda scores: band_stats(scores, offset_cols), cost / math.sqrt(FEAT))
    refined, refine_back = jax.vjp(lambda first_in, second_in: refine(first_in, second_in, valid_f, w_first, w_middle, w_last), coarse, spread)
    grad_coarse, grad_spread = refine_back(grad_out)
    grad_scores = stats_back((grad_coarse, grad_spread))[0]
    grad_cost = (grad_scores / math.sqrt(FEAT)).astype(jnp.bfloat16)

    def grad_row(row_index):
        grad_cost_row = lax.dynamic_index_in_dim(grad_cost, row_index, 0, keepdims=False)

        def tile_step(carry, tile_index):
            left_tile, right_band, start_col = tile_inputs(row_index, tile_index)
            band_vals = lax.dynamic_slice_in_dim(grad_cost_row, (tile_index * W_DEV).astype(jnp.int32), W_DEV, 0)
            band_grad = skew_in(band_vals, band_span)
            left_grad = jnp.dot(band_grad, right_band, preferred_element_type=jnp.float32)
            right_grad = jnp.dot(band_grad.T, left_tile, preferred_element_type=jnp.float32)
            updated = lax.dynamic_slice_in_dim(carry, start_col, band_span, 0) + right_grad
            carry = lax.dynamic_update_slice_in_dim(carry, updated, start_col, 0)
            return (carry, left_grad)
        carry_init = jnp.zeros((pad_left + W, FEAT), jnp.float32)
        final_carry, left_tiles = lax.scan(tile_step, carry_init, tile_ids)
        return (left_tiles.reshape(W, FEAT), final_carry[pad_left:])
    grad_left_all, grad_right_all = lax.map(grad_row, row_ids)
    grad_left_out = jnp.transpose(grad_left_all.astype(jnp.bfloat16), (0, 2, 1))
    grad_right_out = jnp.transpose(grad_right_all.astype(jnp.bfloat16), (0, 2, 1))
    return (refined, grad_left_out, grad_right_out)
```

```python
import functools
import math

import jax
import jax.numpy as jnp
from jax import lax
from jax.experimental import pallas as pl
from jax.experimental.pallas import tpu as pltpu
from jax.sharding import PartitionSpec as P

FEAT = 128
DISP = 256
HALO = 4
LANES = 128
VMEM = 56 * 1024 * 1024
F32, BF16 = jnp.float32, jnp.bfloat16


def from_behind(value, axis, steps):
    count = lax.axis_size(axis)
    first, last = (max(0, -steps), min(count, count - steps))
    return lax.ppermute(value, axis, [(source, source + steps) for source in range(first, last)])


def with_halo(shard, axis, dim, width):
    length = shard.shape[dim]
    before = from_behind(lax.slice_in_dim(shard, length - width, length, axis=dim), axis, 1)
    after = from_behind(lax.slice_in_dim(shard, 0, width, axis=dim), axis, -1)
    return jnp.concatenate([before, shard, after], axis=dim)


def band_of(offset, window_refs, tile):
    window = jnp.concatenate([ref[0] for ref in window_refs], axis=1).astype(F32)
    span = window.shape[1]
    start = span - tile - DISP - offset
    return pltpu.roll(window, span - start, 1)[:, : tile + DISP].astype(BF16)


def skew_out(products):
    tile, span = products.shape
    row_ids = lax.broadcasted_iota(jnp.int32, products.shape, 0)
    for bit in (1, 2, 4):
        products = jnp.where((row_ids & bit) != 0, pltpu.roll(products, span - bit, 1), products)
    pieces = [
        pltpu.roll(products[base : base + 8], span - base - 1, 1)[:, :DISP]
        for base in range(0, tile, 8)
    ]
    return jnp.concatenate(pieces, axis=0)


def skew_in(values, span):
    tile = values.shape[0]
    padded = jnp.concatenate([values, jnp.zeros((tile, span - DISP), values.dtype)], axis=1)
    pieces = [pltpu.roll(padded[base : base + 8], base + 1, 1) for base in range(0, tile, 8)]
    skewed = jnp.concatenate(pieces, axis=0)
    row_ids = lax.broadcasted_iota(jnp.int32, skewed.shape, 0)
    for bit in (1, 2, 4):
        skewed = jnp.where((row_ids & bit) != 0, pltpu.roll(skewed, bit, 1), skewed)
    return skewed


def levels_of(shape):
    return (DISP - 1 - lax.broadcasted_iota(jnp.int32, shape, 1)).astype(F32) / DISP


def cost_kernel(offset_ref, left_ref, far_ref, mid_ref, near_ref, probs_ref, stats_ref):
    row = pl.program_id(0)
    tile = left_ref.shape[2]
    band = band_of(offset_ref[0], (far_ref, mid_ref, near_ref), tile)
    products = lax.dot_general(
        left_ref[0], band, (((0,), (0,)), ((), ())), preferred_element_type=F32
    )
    scores = skew_out(products) / math.sqrt(FEAT)
    exps = jnp.exp(scores - jnp.max(scores, axis=1, keepdims=True))
    probs = exps / jnp.sum(exps, axis=1, keepdims=True)
    levels = levels_of(probs.shape)
    mean = jnp.sum(probs * levels, axis=1, keepdims=True)
    spread = jnp.sum(probs * (levels - mean) ** 2, axis=1, keepdims=True)
    probs_ref[0] = probs
    lanes = lax.broadcasted_iota(jnp.int32, stats_ref.shape, 1)

    @pl.when(row == 0)
    def _():
        stats_ref[...] = jnp.zeros_like(stats_ref)

    stats_ref[...] = jnp.where(
        lanes == row, mean, jnp.where(lanes == row + LANES // 2, spread, stats_ref[...])
    )


def grad_kernel(
    offset_ref, left_ref, far_ref, mid_ref, near_ref, probs_ref, stats_ref, cots_ref,
    left_out, far_out, mid_out, near_out,
):
    row = pl.program_id(0)
    tile = left_ref.shape[2]
    offset = offset_ref[0]
    band = band_of(offset, (far_ref, mid_ref, near_ref), tile)
    lanes = lax.broadcasted_iota(jnp.int32, stats_ref.shape, 1)

    def column(ref, index):
        return jnp.sum(jnp.where(lanes == index, ref[...], 0.0), axis=1, keepdims=True)

    mean = column(stats_ref, row)
    spread = column(stats_ref, row + LANES // 2)
    cot_mean = column(cots_ref, row)
    cot_spread = column(cots_ref, row + LANES // 2)
    probs = probs_ref[0]
    apart = levels_of(probs.shape) - mean
    grad_scores = probs * (cot_mean * apart + cot_spread * (apart * apart - spread))
    grad_cost = (grad_scores / math.sqrt(FEAT)).astype(BF16).astype(F32)
    skewed = skew_in(grad_cost, tile + DISP).astype(BF16)
    left_grad = lax.dot_general(
        band, skewed, (((1,), (1,)), ((), ())), preferred_element_type=F32
    )
    left_out[0] = left_grad.astype(BF16)
    right_grad = jnp.dot(left_ref[0], skewed, preferred_element_type=F32)
    span = 3 * tile
    padded = jnp.concatenate(
        [right_grad, jnp.zeros((right_grad.shape[0], span - tile - DISP), F32)], axis=1
    )
    moved = pltpu.roll(padded, span - tile - DISP - offset, 1)
    far_out[0] = moved[:, :tile].astype(BF16)
    mid_out[0] = moved[:, tile : 2 * tile]
    near_out[0] = moved[:, 2 * tile :]


def split_halves(values):
    upper = values.astype(BF16)
    return upper, (values - upper.astype(F32)).astype(BF16)


def weight_side(matrix, rows, depth):
    padded = jnp.pad(matrix, ((0, rows - matrix.shape[0]), (0, depth - matrix.shape[1])))
    upper, lower = split_halves(padded)
    return jnp.concatenate([upper, upper, lower], axis=1)


def field_side(values):
    upper, lower = split_halves(values)
    return jnp.concatenate([upper, lower, upper], axis=0)


def refine_kernel(
    stride, fields_ref, first_ref, middle_ref, last_ref, last_back_ref, middle_back_ref,
    first_back_ref, out_ref, slope_one, slope_two, packed, spread_out,
):
    cells = fields_ref.shape[1]
    chans = slope_one.shape[0]
    taps = [(a - 1) * stride + (b - 1) for a in range(3) for b in range(3)]

    def ahead(values, steps):
        return values if steps == 0 else pltpu.roll(values, -steps % cells, 1)

    def gather(rows, sign, depth):
        parts = [ahead(rows, sign * tap) for tap in taps]
        count = sum(part.shape[0] for part in parts)
        parts.append(jnp.zeros((depth - count, cells), F32))
        return jnp.concatenate(parts, axis=0)

    def product(weights_ref, values):
        return jnp.dot(weights_ref[...], field_side(values), preferred_element_type=F32)

    def scatter(rows_of, sign):
        total = None
        for index, tap in enumerate(taps):
            part = ahead(rows_of(index), sign * tap)
            total = part if total is None else total + part
        return total

    def silu_parts(values):
        sig = 1.0 / (1.0 + jnp.exp(-values))
        return values * sig, sig * (1.0 + values * (1.0 - sig))

    def middle(weights_ref, sign):
        spread_out[...] = jnp.dot(weights_ref[...], packed[...], preferred_element_type=F32)
        return scatter(lambda index: spread_out[index * chans : (index + 1) * chans], sign)

    inside = fields_ref[3:4]
    hidden, slope = silu_parts(product(first_ref, gather(fields_ref[0:2], 1, chans)))
    slope_one[...] = slope * inside
    packed[...] = field_side(hidden * inside)
    hidden, slope = silu_parts(middle(middle_ref, 1))
    slope_two[...] = slope * inside
    rows = product(last_ref, hidden * inside)
    out_ref[0:1] = scatter(lambda index: rows[index : index + 1], 1)
    grad_two = product(last_back_ref, gather(fields_ref[2:3], -1, chans)) * slope_two[...]
    packed[...] = field_side(grad_two)
    grad_one = middle(middle_back_ref, -1) * slope_one[...]
    rows = product(first_back_ref, grad_one)
    out_ref[1:3] = scatter(lambda index: rows[2 * index : 2 * index + 2], -1)
    out_ref[3:8] = jnp.zeros((5, cells), F32)


def refine(fields, w_first, w_middle, w_last):
    count, rows, cols = fields.shape
    cells = rows * cols
    padded_cells = -(-cells // 256) * 256
    flat = jnp.pad(fields.reshape(count, cells), ((0, 8 - count), (0, padded_cells - cells)))
    chans = w_middle.shape[2]
    first = weight_side(w_first.transpose(2, 0, 1, 3).reshape(chans, -1), chans, chans)
    middle = weight_side(w_middle.reshape(-1, chans), 9 * chans, chans)
    last = weight_side(w_last.reshape(9, chans), 16, chans)
    last_back = weight_side(w_last.reshape(9, chans).T, chans, chans)
    middle_back = weight_side(w_middle.transpose(0, 1, 3, 2).reshape(-1, chans), 9 * chans, chans)
    first_back = weight_side(w_first.transpose(0, 1, 3, 2).reshape(-1, chans), chans, chans)
    out = pl.pallas_call(
        functools.partial(refine_kernel, cols),
        out_shape=jax.ShapeDtypeStruct((8, padded_cells), F32),
        in_specs=[pl.BlockSpec(memory_space=pltpu.VMEM)] * 7,
        out_specs=pl.BlockSpec(memory_space=pltpu.VMEM),
        scratch_shapes=[
            pltpu.VMEM((chans, padded_cells), F32),
            pltpu.VMEM((chans, padded_cells), F32),
            pltpu.VMEM((3 * chans, padded_cells), BF16),
            pltpu.VMEM((9 * chans, padded_cells), F32),
        ],
        compiler_params=pltpu.CompilerParams(vmem_limit_bytes=VMEM),
        name="refine",
    )(flat, first, middle, last, last_back, middle_back, first_back)
    return out[:3, :cells].reshape(3, rows, cols)


def row_block(array):
    return pl.BlockSpec((1,) + array.shape[1:], lambda row: (row, 0, 0))


def whole_block(shape):
    return pl.BlockSpec(shape, lambda row: (0, 0))


def match(offsets, left, window):
    rows, _, tile = left.shape
    probs = jax.ShapeDtypeStruct((rows, tile, DISP), F32)
    stats = jax.ShapeDtypeStruct((tile, LANES), F32)
    return pl.pallas_call(
        cost_kernel,
        grid=(rows,),
        in_specs=[pl.BlockSpec(memory_space=pltpu.SMEM), row_block(left)]
        + [row_block(part) for part in window],
        out_specs=[row_block(probs), whole_block(stats.shape)],
        out_shape=[probs, stats],
        compiler_params=pltpu.CompilerParams(vmem_limit_bytes=VMEM),
        name="match",
    )(offsets, left, *window)


def match_grads(offsets, left, window, probs, stats, cots):
    rows, feats, tile = left.shape
    narrow = jax.ShapeDtypeStruct((rows, feats, tile), BF16)
    wide = jax.ShapeDtypeStruct((rows, feats, tile), F32)
    return pl.pallas_call(
        grad_kernel,
        grid=(rows,),
        in_specs=[pl.BlockSpec(memory_space=pltpu.SMEM), row_block(left)]
        + [row_block(part) for part in window]
        + [row_block(probs), whole_block(stats.shape), whole_block(cots.shape)],
        out_specs=[row_block(left)] * 4,
        out_shape=[narrow, narrow, wide, wide],
        compiler_params=pltpu.CompilerParams(vmem_limit_bytes=VMEM),
        name="match_grads",
    )(offsets, left, *window, probs, stats, cots)


def to_rows(array, rows_dim, other_dim):
    return lax.all_to_all(array, "ch", rows_dim, other_dim, tiled=True)


def shards(left_feat, right_feat, offsets, valid, w_first, w_middle, w_last, grad_out):
    near = to_rows(right_feat, 0, 1)
    mid = from_behind(near, "col", 1)
    left = to_rows(left_feat, 0, 1)
    keep_cols = valid.astype(F32)
    planes = to_rows(jnp.stack([keep_cols, grad_out * keep_cols]), 1, 2)
    keep, grad_top = planes[0], planes[1]
    far = from_behind(mid, "col", 1)
    window = (far, mid, near)
    probs, stats = match(offsets, left, window)
    rows, cols = keep.shape
    flipped = stats.T
    coarse = offsets[0].astype(F32) / DISP + flipped[:rows]
    spread = flipped[LANES // 2 : LANES // 2 + rows]
    fields = jnp.stack([coarse * keep, spread * keep, grad_top])
    fields = with_halo(fields, ("row", "ch"), 1, HALO)
    fields = with_halo(fields, "col", 2, HALO)
    row_at = lax.axis_index(("row", "ch")) * rows - HALO + jnp.arange(rows + 2 * HALO)
    col_at = lax.axis_index("col") * cols - HALO + jnp.arange(cols + 2 * HALO)
    row_in = (row_at >= 0) & (row_at < rows * lax.axis_size(("row", "ch")))
    col_in = (col_at >= 0) & (col_at < cols * lax.axis_size("col"))
    inside = (row_in[:, None] & col_in[None, :]).astype(F32)
    results = refine(jnp.concatenate([fields, inside[None]]), w_first, w_middle, w_last)
    results = results[:, HALO : HALO + rows, HALO : HALO + cols]
    refined = keep * (coarse + results[0])
    gap = jnp.zeros((LANES // 2 - rows, cols), F32)
    cots = jnp.concatenate(
        [grad_top + results[1] * keep, gap, results[2] * keep, gap]
    ).T
    grad_left, far_grad, mid_grad, near_grad = match_grads(
        offsets, left, window, probs, stats, cots
    )
    carried = from_behind(far_grad, "col", -1)
    carried = from_behind((mid_grad + carried.astype(F32)).astype(BF16), "col", -1)
    grad_right = (near_grad + carried.astype(F32)).astype(BF16)
    return (
        to_rows(refined, 1, 0),
        to_rows(grad_left, 1, 0),
        to_rows(grad_right, 1, 0),
    )


def solution(mesh):
    placed = (
        P(("slab", "row"), "ch", "col"),
        P(("slab", "row"), "ch", "col"),
        P(("slab", "col")),
        P(("slab", "row"), ("col", "ch")),
        P(),
        P(),
        P(),
        P(("slab", "row"), ("col", "ch")),
    )
    return jax.shard_map(
        shards,
        mesh=mesh,
        in_specs=placed,
        out_specs=(
            P(("slab", "row"), ("col", "ch")),
            P(("slab", "row"), "ch", "col"),
            P(("slab", "row"), "ch", "col"),
        ),
        check_vma=False,
    )
```

```python
import functools
import math

import jax
import jax.numpy as jnp
from jax import lax
from jax.experimental import pallas as pl
from jax.experimental.pallas import tpu as pltpu
from jax.sharding import PartitionSpec as P

FEAT = 128
DISP = 256
HALO = 4
LANES = 128
CHUNKS = 2
VMEM = 56 * 1024 * 1024
F32, BF16 = jnp.float32, jnp.bfloat16


def from_behind(value, axis, steps):
    count = lax.axis_size(axis)
    first, last = (max(0, -steps), min(count, count - steps))
    return lax.ppermute(value, axis, [(source, source + steps) for source in range(first, last)])


def with_halo(shard, axis, dim, width):
    length = shard.shape[dim]
    before = from_behind(lax.slice_in_dim(shard, length - width, length, axis=dim), axis, 1)
    after = from_behind(lax.slice_in_dim(shard, 0, width, axis=dim), axis, -1)
    return jnp.concatenate([before, shard, after], axis=dim)


def band_of(offset, window_refs, tile):
    window = jnp.concatenate([ref[0] for ref in window_refs], axis=1).astype(F32)
    span = window.shape[1]
    start = span - tile - DISP - offset
    return pltpu.roll(window, span - start, 1)[:, : tile + DISP].astype(BF16)


def skew_out(products):
    tile, span = products.shape
    row_ids = lax.broadcasted_iota(jnp.int32, products.shape, 0)
    for bit in (1, 2, 4):
        products = jnp.where((row_ids & bit) != 0, pltpu.roll(products, span - bit, 1), products)
    pieces = [
        pltpu.roll(products[base : base + 8], span - base - 1, 1)[:, :DISP]
        for base in range(0, tile, 8)
    ]
    return jnp.concatenate(pieces, axis=0)


def skew_in(values, span):
    tile = values.shape[0]
    padded = jnp.concatenate([values, jnp.zeros((tile, span - DISP), values.dtype)], axis=1)
    pieces = [pltpu.roll(padded[base : base + 8], base + 1, 1) for base in range(0, tile, 8)]
    skewed = jnp.concatenate(pieces, axis=0)
    row_ids = lax.broadcasted_iota(jnp.int32, skewed.shape, 0)
    for bit in (1, 2, 4):
        skewed = jnp.where((row_ids & bit) != 0, pltpu.roll(skewed, bit, 1), skewed)
    return skewed


def levels_of(shape):
    return (DISP - 1 - lax.broadcasted_iota(jnp.int32, shape, 1)).astype(F32) / DISP


def cost_kernel(offset_ref, left_ref, far_ref, mid_ref, near_ref, probs_ref, stats_ref):
    row = pl.program_id(0)
    tile = left_ref.shape[2]
    band = band_of(offset_ref[0], (far_ref, mid_ref, near_ref), tile)
    products = lax.dot_general(
        left_ref[0], band, (((0,), (0,)), ((), ())), preferred_element_type=F32
    )
    scores = skew_out(products) / math.sqrt(FEAT)
    exps = jnp.exp(scores - jnp.max(scores, axis=1, keepdims=True))
    probs = exps / jnp.sum(exps, axis=1, keepdims=True)
    levels = levels_of(probs.shape)
    mean = jnp.sum(probs * levels, axis=1, keepdims=True)
    spread = jnp.sum(probs * (levels - mean) ** 2, axis=1, keepdims=True)
    probs_ref[0] = probs
    lanes = lax.broadcasted_iota(jnp.int32, stats_ref.shape, 1)

    @pl.when(row == 0)
    def _():
        stats_ref[...] = jnp.zeros_like(stats_ref)

    stats_ref[...] = jnp.where(
        lanes == row, mean, jnp.where(lanes == row + LANES // 2, spread, stats_ref[...])
    )


def grad_kernel(
    base, offset_ref, left_ref, far_ref, mid_ref, near_ref, probs_ref, stats_ref, cots_ref,
    left_out, far_out, mid_out, near_out,
):
    row = pl.program_id(0)
    tile = left_ref.shape[2]
    offset = offset_ref[0]
    band = band_of(offset, (far_ref, mid_ref, near_ref), tile)
    lanes = lax.broadcasted_iota(jnp.int32, stats_ref.shape, 1)

    def column(ref, index):
        return jnp.sum(jnp.where(lanes == index, ref[...], 0.0), axis=1, keepdims=True)

    mean = column(stats_ref, row)
    spread = column(stats_ref, row + LANES // 2)
    cot_mean = column(cots_ref, row + base)
    cot_spread = column(cots_ref, row + base + LANES // 2)
    probs = probs_ref[0]
    apart = levels_of(probs.shape) - mean
    grad_scores = probs * (cot_mean * apart + cot_spread * (apart * apart - spread))
    grad_cost = (grad_scores / math.sqrt(FEAT)).astype(BF16).astype(F32)
    skewed = skew_in(grad_cost, tile + DISP).astype(BF16)
    left_grad = lax.dot_general(
        band, skewed, (((1,), (1,)), ((), ())), preferred_element_type=F32
    )
    left_out[0] = left_grad.astype(BF16)
    right_grad = jnp.dot(left_ref[0], skewed, preferred_element_type=F32)
    span = 3 * tile
    padded = jnp.concatenate(
        [right_grad, jnp.zeros((right_grad.shape[0], span - tile - DISP), F32)], axis=1
    )
    moved = pltpu.roll(padded, span - tile - DISP - offset, 1)
    far_out[0] = moved[:, :tile].astype(BF16)
    mid_out[0] = moved[:, tile : 2 * tile]
    near_out[0] = moved[:, 2 * tile :]


def split_halves(values):
    upper = values.astype(BF16)
    return upper, (values - upper.astype(F32)).astype(BF16)


def weight_side(matrix, rows, depth):
    padded = jnp.pad(matrix, ((0, rows - matrix.shape[0]), (0, depth - matrix.shape[1])))
    upper, lower = split_halves(padded)
    return jnp.concatenate([upper, upper, lower], axis=1)


def field_side(values):
    upper, lower = split_halves(values)
    return jnp.concatenate([upper, lower, upper], axis=0)


def refine_kernel(
    stride, fields_ref, first_ref, middle_ref, last_ref, last_back_ref, middle_back_ref,
    first_back_ref, out_ref, slope_one, slope_two, packed, spread_out,
):
    cells = fields_ref.shape[1]
    chans = slope_one.shape[0]
    taps = [(a - 1) * stride + (b - 1) for a in range(3) for b in range(3)]

    def ahead(values, steps):
        return values if steps == 0 else pltpu.roll(values, -steps % cells, 1)

    def gather(rows, sign, depth):
        parts = [ahead(rows, sign * tap) for tap in taps]
        count = sum(part.shape[0] for part in parts)
        parts.append(jnp.zeros((depth - count, cells), F32))
        return jnp.concatenate(parts, axis=0)

    def product(weights_ref, values):
        return jnp.dot(weights_ref[...], field_side(values), preferred_element_type=F32)

    def scatter(rows_of, sign):
        total = None
        for index, tap in enumerate(taps):
            part = ahead(rows_of(index), sign * tap)
            total = part if total is None else total + part
        return total

    def silu_parts(values):
        sig = 1.0 / (1.0 + jnp.exp(-values))
        return values * sig, sig * (1.0 + values * (1.0 - sig))

    def middle(weights_ref, sign):
        spread_out[...] = jnp.dot(weights_ref[...], packed[...], preferred_element_type=F32)
        return scatter(lambda index: spread_out[index * chans : (index + 1) * chans], sign)

    inside = fields_ref[3:4]
    hidden, slope = silu_parts(product(first_ref, gather(fields_ref[0:2], 1, chans)))
    slope_one[...] = slope * inside
    packed[...] = field_side(hidden * inside)
    hidden, slope = silu_parts(middle(middle_ref, 1))
    slope_two[...] = slope * inside
    rows = product(last_ref, hidden * inside)
    out_ref[0:1] = scatter(lambda index: rows[index : index + 1], 1)
    grad_two = product(last_back_ref, gather(fields_ref[2:3], -1, chans)) * slope_two[...]
    packed[...] = field_side(grad_two)
    grad_one = middle(middle_back_ref, -1) * slope_one[...]
    rows = product(first_back_ref, grad_one)
    out_ref[1:3] = scatter(lambda index: rows[2 * index : 2 * index + 2], -1)
    out_ref[3:8] = jnp.zeros((5, cells), F32)


def refine(fields, w_first, w_middle, w_last):
    count, rows, cols = fields.shape
    cells = rows * cols
    padded_cells = -(-cells // 256) * 256
    flat = jnp.pad(fields.reshape(count, cells), ((0, 8 - count), (0, padded_cells - cells)))
    chans = w_middle.shape[2]
    first = weight_side(w_first.transpose(2, 0, 1, 3).reshape(chans, -1), chans, chans)
    middle = weight_side(w_middle.reshape(-1, chans), 9 * chans, chans)
    last = weight_side(w_last.reshape(9, chans), 16, chans)
    last_back = weight_side(w_last.reshape(9, chans).T, chans, chans)
    middle_back = weight_side(w_middle.transpose(0, 1, 3, 2).reshape(-1, chans), 9 * chans, chans)
    first_back = weight_side(w_first.transpose(0, 1, 3, 2).reshape(-1, chans), chans, chans)
    out = pl.pallas_call(
        functools.partial(refine_kernel, cols),
        out_shape=jax.ShapeDtypeStruct((8, padded_cells), F32),
        in_specs=[pl.BlockSpec(memory_space=pltpu.VMEM)] * 7,
        out_specs=pl.BlockSpec(memory_space=pltpu.VMEM),
        scratch_shapes=[
            pltpu.VMEM((chans, padded_cells), F32),
            pltpu.VMEM((chans, padded_cells), F32),
            pltpu.VMEM((3 * chans, padded_cells), BF16),
            pltpu.VMEM((9 * chans, padded_cells), F32),
        ],
        compiler_params=pltpu.CompilerParams(vmem_limit_bytes=VMEM),
        name="refine",
    )(flat, first, middle, last, last_back, middle_back, first_back)
    return out[:3, :cells].reshape(3, rows, cols)


def row_block(array, base=0):
    return pl.BlockSpec((1,) + array.shape[1:], lambda row: (row + base, 0, 0))


def whole_block(shape):
    return pl.BlockSpec(shape, lambda row: (0, 0))


def cost_of(rows, tile):
    return pl.CostEstimate(
        flops=rows * tile * (3 * tile) * FEAT * 2,
        bytes_accessed=rows * tile * DISP * 64,
        transcendentals=rows * tile * DISP,
    )


def match(offsets, left, base, window):
    tile = left.shape[2]
    rows = window[0].shape[0]
    probs = jax.ShapeDtypeStruct((rows, tile, DISP), F32)
    stats = jax.ShapeDtypeStruct((tile, LANES), F32)
    return pl.pallas_call(
        cost_kernel,
        grid=(rows,),
        in_specs=[pl.BlockSpec(memory_space=pltpu.SMEM), row_block(left, base)]
        + [row_block(part) for part in window],
        out_specs=[row_block(probs), whole_block(stats.shape)],
        out_shape=[probs, stats],
        compiler_params=pltpu.CompilerParams(vmem_limit_bytes=VMEM),
        cost_estimate=cost_of(rows, tile),
        name="match",
    )(offsets, left, *window)


def match_grads(offsets, left, base, window, probs, stats, cots):
    feats, tile = left.shape[1:]
    rows = window[0].shape[0]
    narrow = jax.ShapeDtypeStruct((rows, feats, tile), BF16)
    wide = jax.ShapeDtypeStruct((rows, feats, tile), F32)
    return pl.pallas_call(
        functools.partial(grad_kernel, base),
        grid=(rows,),
        in_specs=[pl.BlockSpec(memory_space=pltpu.SMEM), row_block(left, base)]
        + [row_block(part) for part in window]
        + [row_block(probs), whole_block(stats.shape), whole_block(cots.shape)],
        out_specs=[row_block(narrow)] * 4,
        out_shape=[narrow, narrow, wide, wide],
        compiler_params=pltpu.CompilerParams(vmem_limit_bytes=VMEM),
        cost_estimate=cost_of(rows, tile),
        name="match_grads",
    )(offsets, left, *window, probs, stats, cots)


def to_rows(array, rows_dim, other_dim):
    return lax.all_to_all(array, "ch", rows_dim, other_dim, tiled=True)


def chunk_count(rows):
    return CHUNKS if rows % CHUNKS == 0 else 1


def shards(left_feat, right_feat, offsets, valid, w_first, w_middle, w_last, grad_out):
    whole_near = to_rows(right_feat, 0, 1)
    left_feat, valid, grad_out, whole_near = lax.optimization_barrier(
        (left_feat, valid, grad_out, whole_near)
    )
    rows, _, cols = whole_near.shape
    chunks = chunk_count(rows)
    step = rows // chunks
    near = [whole_near[index * step : (index + 1) * step] for index in range(chunks)]
    mid = [from_behind(part, "col", 1) for part in near]
    left = to_rows(left_feat, 0, 1)
    keep_cols = valid.astype(F32)
    planes = to_rows(jnp.stack([keep_cols, grad_out * keep_cols]), 1, 2)
    keep, grad_top = planes[0], planes[1]
    far = [from_behind(part, "col", 1) for part in mid]
    windows = list(zip(far, mid, near))
    matched = [
        match(offsets, left, index * step, window) for index, window in enumerate(windows)
    ]
    flipped = [stats.T for _, stats in matched]
    mean_level = jnp.concatenate([part[:step] for part in flipped])
    spread = jnp.concatenate([part[LANES // 2 : LANES // 2 + step] for part in flipped])
    coarse = offsets[0].astype(F32) / DISP + mean_level
    fields = jnp.stack([coarse * keep, spread * keep, grad_top])
    fields = with_halo(fields, ("row", "ch"), 1, HALO)
    fields = with_halo(fields, "col", 2, HALO)
    row_at = lax.axis_index(("row", "ch")) * rows - HALO + jnp.arange(rows + 2 * HALO)
    col_at = lax.axis_index("col") * cols - HALO + jnp.arange(cols + 2 * HALO)
    row_in = (row_at >= 0) & (row_at < rows * lax.axis_size(("row", "ch")))
    col_in = (col_at >= 0) & (col_at < cols * lax.axis_size("col"))
    inside = (row_in[:, None] & col_in[None, :]).astype(F32)
    results = refine(jnp.concatenate([fields, inside[None]]), w_first, w_middle, w_last)
    results = results[:, HALO : HALO + rows, HALO : HALO + cols]
    refined = keep * (coarse + results[0])
    gap = jnp.zeros((LANES // 2 - rows, cols), F32)
    cots = jnp.concatenate(
        [grad_top + results[1] * keep, gap, results[2] * keep, gap]
    ).T
    left_parts, right_parts = [], []
    for index, (window, (probs, stats)) in enumerate(zip(windows, matched)):
        grad_left, far_grad, mid_grad, near_grad = match_grads(
            offsets, left, index * step, window, probs, stats, cots
        )
        carried = from_behind(far_grad, "col", -1)
        carried = from_behind((mid_grad + carried.astype(F32)).astype(BF16), "col", -1)
        left_parts.append(to_rows(grad_left, 1, 0))
        right_parts.append(to_rows((near_grad + carried.astype(F32)).astype(BF16), 1, 0))

    def assemble(parts):
        parts = [part.reshape((2, step) + part.shape[1:]) for part in parts]
        stacked = jnp.stack(parts, axis=1)
        return stacked.reshape((2 * rows,) + stacked.shape[3:])

    return (to_rows(refined, 1, 0), assemble(left_parts), assemble(right_parts))


def solution(mesh):
    placed = (
        P(("slab", "row"), "ch", "col"),
        P(("slab", "row"), "ch", "col"),
        P(("slab", "col")),
        P(("slab", "row"), ("col", "ch")),
        P(),
        P(),
        P(),
        P(("slab", "row"), ("col", "ch")),
    )
    return jax.shard_map(
        shards,
        mesh=mesh,
        in_specs=placed,
        out_specs=(
            P(("slab", "row"), ("col", "ch")),
            P(("slab", "row"), "ch", "col"),
            P(("slab", "row"), "ch", "col"),
        ),
        check_vma=False,
    )
```

```python
import functools
import math

import jax
import jax.numpy as jnp
from jax import lax
from jax.experimental import pallas as pl
from jax.experimental.pallas import tpu as pltpu
from jax.sharding import PartitionSpec as P

FEAT = 128
DISP = 256
HALO = 4
LANES = 128
CHUNKS = 2
VMEM = 56 * 1024 * 1024
F32, BF16 = jnp.float32, jnp.bfloat16


def from_behind(value, axis, steps):
    count = lax.axis_size(axis)
    first, last = (max(0, -steps), min(count, count - steps))
    return lax.ppermute(value, axis, [(source, source + steps) for source in range(first, last)])


def with_halo(shard, axis, dim, width):
    length = shard.shape[dim]
    before = from_behind(lax.slice_in_dim(shard, length - width, length, axis=dim), axis, 1)
    after = from_behind(lax.slice_in_dim(shard, 0, width, axis=dim), axis, -1)
    return jnp.concatenate([before, shard, after], axis=dim)


def band_of(offset, window_refs, tile):
    window = jnp.concatenate([ref[0] for ref in window_refs], axis=1).astype(F32)
    span = window.shape[1]
    start = span - tile - DISP - offset
    return pltpu.roll(window, span - start, 1)[:, : tile + DISP].astype(BF16)


def skew_out(products):
    tile, span = products.shape
    row_ids = lax.broadcasted_iota(jnp.int32, products.shape, 0)
    for bit in (1, 2, 4):
        products = jnp.where((row_ids & bit) != 0, pltpu.roll(products, span - bit, 1), products)
    pieces = [
        pltpu.roll(products[base : base + 8], span - base - 1, 1)[:, :DISP]
        for base in range(0, tile, 8)
    ]
    return jnp.concatenate(pieces, axis=0)


def skew_in(values, span):
    tile = values.shape[0]
    padded = jnp.concatenate([values, jnp.zeros((tile, span - DISP), values.dtype)], axis=1)
    pieces = [pltpu.roll(padded[base : base + 8], base + 1, 1) for base in range(0, tile, 8)]
    skewed = jnp.concatenate(pieces, axis=0)
    row_ids = lax.broadcasted_iota(jnp.int32, skewed.shape, 0)
    for bit in (1, 2, 4):
        skewed = jnp.where((row_ids & bit) != 0, pltpu.roll(skewed, bit, 1), skewed)
    return skewed


def levels_of(shape):
    return (DISP - 1 - lax.broadcasted_iota(jnp.int32, shape, 1)).astype(F32) / DISP


def cost_kernel(offset_ref, left_ref, far_ref, mid_ref, near_ref, probs_ref, stats_ref):
    row = pl.program_id(0)
    tile = left_ref.shape[2]
    band = band_of(offset_ref[0], (far_ref, mid_ref, near_ref), tile)
    products = lax.dot_general(
        left_ref[0], band, (((0,), (0,)), ((), ())), preferred_element_type=F32
    )
    scores = skew_out(products) / math.sqrt(FEAT)
    exps = jnp.exp(scores - jnp.max(scores, axis=1, keepdims=True))
    probs = exps / jnp.sum(exps, axis=1, keepdims=True)
    levels = levels_of(probs.shape)
    mean = jnp.sum(probs * levels, axis=1, keepdims=True)
    spread = jnp.sum(probs * (levels - mean) ** 2, axis=1, keepdims=True)
    probs_ref[0] = probs
    lanes = lax.broadcasted_iota(jnp.int32, stats_ref.shape, 1)

    @pl.when(row == 0)
    def _():
        stats_ref[...] = jnp.zeros_like(stats_ref)

    stats_ref[...] = jnp.where(
        lanes == row, mean, jnp.where(lanes == row + LANES // 2, spread, stats_ref[...])
    )


def grad_kernel(
    base, offset_ref, left_ref, far_ref, mid_ref, near_ref, probs_ref, stats_ref, cots_ref,
    left_out, far_out, mid_out, near_out,
):
    row = pl.program_id(0)
    tile = left_ref.shape[2]
    offset = offset_ref[0]
    band = band_of(offset, (far_ref, mid_ref, near_ref), tile)
    lanes = lax.broadcasted_iota(jnp.int32, stats_ref.shape, 1)

    def column(ref, index):
        return jnp.sum(jnp.where(lanes == index, ref[...], 0.0), axis=1, keepdims=True)

    mean = column(stats_ref, row)
    spread = column(stats_ref, row + LANES // 2)
    cot_mean = column(cots_ref, row + base)
    cot_spread = column(cots_ref, row + base + LANES // 2)
    probs = probs_ref[0]
    apart = levels_of(probs.shape) - mean
    grad_scores = probs * (cot_mean * apart + cot_spread * (apart * apart - spread))
    grad_cost = (grad_scores / math.sqrt(FEAT)).astype(BF16).astype(F32)
    skewed = skew_in(grad_cost, tile + DISP).astype(BF16)
    left_grad = lax.dot_general(
        band, skewed, (((1,), (1,)), ((), ())), preferred_element_type=F32
    )
    left_out[0] = left_grad.astype(BF16)
    right_grad = jnp.dot(left_ref[0], skewed, preferred_element_type=F32)
    span = 3 * tile
    padded = jnp.concatenate(
        [right_grad, jnp.zeros((right_grad.shape[0], span - tile - DISP), F32)], axis=1
    )
    moved = pltpu.roll(padded, span - tile - DISP - offset, 1)
    far_out[0] = moved[:, :tile].astype(BF16)
    mid_out[0] = moved[:, tile : 2 * tile]
    near_out[0] = moved[:, 2 * tile :]


def split_halves(values):
    upper = values.astype(BF16)
    return upper, (values - upper.astype(F32)).astype(BF16)


def weight_side(matrix, rows, depth):
    padded = jnp.pad(matrix, ((0, rows - matrix.shape[0]), (0, depth - matrix.shape[1])))
    upper, lower = split_halves(padded)
    return jnp.concatenate([upper, upper, lower], axis=1)


def field_side(values):
    upper, lower = split_halves(values)
    return jnp.concatenate([upper, lower, upper], axis=0)


def refine_kernel(
    stride, fields_ref, first_ref, middle_ref, last_ref, last_back_ref, middle_back_ref,
    first_back_ref, out_ref, slope_one, slope_two, packed, spread_out,
):
    cells = fields_ref.shape[1]
    chans = slope_one.shape[0]
    taps = [(a - 1) * stride + (b - 1) for a in range(3) for b in range(3)]

    def ahead(values, steps):
        return values if steps == 0 else pltpu.roll(values, -steps % cells, 1)

    def gather(rows, sign, depth):
        parts = [ahead(rows, sign * tap) for tap in taps]
        count = sum(part.shape[0] for part in parts)
        parts.append(jnp.zeros((depth - count, cells), F32))
        return jnp.concatenate(parts, axis=0)

    def product(weights_ref, values):
        return jnp.dot(weights_ref[...], field_side(values), preferred_element_type=F32)

    def scatter(rows_of, sign):
        total = None
        for index, tap in enumerate(taps):
            part = ahead(rows_of(index), sign * tap)
            total = part if total is None else total + part
        return total

    def silu_parts(values):
        sig = 1.0 / (1.0 + jnp.exp(-values))
        return values * sig, sig * (1.0 + values * (1.0 - sig))

    def middle(weights_ref, sign):
        spread_out[...] = jnp.dot(weights_ref[...], packed[...], preferred_element_type=F32)
        return scatter(lambda index: spread_out[index * chans : (index + 1) * chans], sign)

    inside = fields_ref[3:4]
    hidden, slope = silu_parts(product(first_ref, gather(fields_ref[0:2], 1, chans)))
    slope_one[...] = slope * inside
    packed[...] = field_side(hidden * inside)
    hidden, slope = silu_parts(middle(middle_ref, 1))
    slope_two[...] = slope * inside
    rows = product(last_ref, hidden * inside)
    out_ref[0:1] = scatter(lambda index: rows[index : index + 1], 1)
    grad_two = product(last_back_ref, gather(fields_ref[2:3], -1, chans)) * slope_two[...]
    packed[...] = field_side(grad_two)
    grad_one = middle(middle_back_ref, -1) * slope_one[...]
    rows = product(first_back_ref, grad_one)
    out_ref[1:3] = scatter(lambda index: rows[2 * index : 2 * index + 2], -1)
    out_ref[3:8] = jnp.zeros((5, cells), F32)


def refine(fields, w_first, w_middle, w_last):
    count, rows, cols = fields.shape
    cells = rows * cols
    padded_cells = -(-cells // 256) * 256
    flat = jnp.pad(fields.reshape(count, cells), ((0, 8 - count), (0, padded_cells - cells)))
    chans = w_middle.shape[2]
    first = weight_side(w_first.transpose(2, 0, 1, 3).reshape(chans, -1), chans, chans)
    middle = weight_side(w_middle.reshape(-1, chans), 9 * chans, chans)
    last = weight_side(w_last.reshape(9, chans), 16, chans)
    last_back = weight_side(w_last.reshape(9, chans).T, chans, chans)
    middle_back = weight_side(w_middle.transpose(0, 1, 3, 2).reshape(-1, chans), 9 * chans, chans)
    first_back = weight_side(w_first.transpose(0, 1, 3, 2).reshape(-1, chans), chans, chans)
    out = pl.pallas_call(
        functools.partial(refine_kernel, cols),
        out_shape=jax.ShapeDtypeStruct((8, padded_cells), F32),
        in_specs=[pl.BlockSpec(memory_space=pltpu.VMEM)] * 7,
        out_specs=pl.BlockSpec(memory_space=pltpu.VMEM),
        scratch_shapes=[
            pltpu.VMEM((chans, padded_cells), F32),
            pltpu.VMEM((chans, padded_cells), F32),
            pltpu.VMEM((3 * chans, padded_cells), BF16),
            pltpu.VMEM((9 * chans, padded_cells), F32),
        ],
        compiler_params=pltpu.CompilerParams(vmem_limit_bytes=VMEM),
        name="refine",
    )(flat, first, middle, last, last_back, middle_back, first_back)
    return out[:3, :cells].reshape(3, rows, cols)


def row_block(array, base=0):
    return pl.BlockSpec((1,) + array.shape[1:], lambda row: (row + base, 0, 0))


def whole_block(shape):
    return pl.BlockSpec(shape, lambda row: (0, 0))


def cost_of(rows, tile):
    return pl.CostEstimate(
        flops=rows * tile * (3 * tile) * FEAT * 2,
        bytes_accessed=rows * tile * DISP * 64,
        transcendentals=rows * tile * DISP,
    )


def match(offsets, left, base, window):
    tile = left.shape[2]
    rows = window[0].shape[0]
    probs = jax.ShapeDtypeStruct((rows, tile, DISP), F32)
    stats = jax.ShapeDtypeStruct((tile, LANES), F32)
    return pl.pallas_call(
        cost_kernel,
        grid=(rows,),
        in_specs=[pl.BlockSpec(memory_space=pltpu.SMEM), row_block(left, base)]
        + [row_block(part) for part in window[:2]]
        + [row_block(window[2], base)],
        out_specs=[row_block(probs), whole_block(stats.shape)],
        out_shape=[probs, stats],
        compiler_params=pltpu.CompilerParams(vmem_limit_bytes=VMEM),
        cost_estimate=cost_of(rows, tile),
        name="match",
    )(offsets, left, *window)


def match_grads(offsets, left, base, window, probs, stats, cots):
    feats, tile = left.shape[1:]
    rows = window[0].shape[0]
    narrow = jax.ShapeDtypeStruct((rows, feats, tile), BF16)
    wide = jax.ShapeDtypeStruct((rows, feats, tile), F32)
    return pl.pallas_call(
        functools.partial(grad_kernel, base),
        grid=(rows,),
        in_specs=[pl.BlockSpec(memory_space=pltpu.SMEM), row_block(left, base)]
        + [row_block(part) for part in window[:2]]
        + [row_block(window[2], base)]
        + [row_block(probs), whole_block(stats.shape), whole_block(cots.shape)],
        out_specs=[row_block(narrow)] * 4,
        out_shape=[narrow, narrow, wide, wide],
        compiler_params=pltpu.CompilerParams(vmem_limit_bytes=VMEM),
        cost_estimate=cost_of(rows, tile),
        name="match_grads",
    )(offsets, left, *window, probs, stats, cots)


def to_rows(array, rows_dim, other_dim):
    return lax.all_to_all(array, "ch", rows_dim, other_dim, tiled=True)


def chunk_count(rows):
    return CHUNKS if rows % CHUNKS == 0 else 1


def shards(left_feat, right_feat, offsets, valid, w_first, w_middle, w_last, grad_out):
    double_rows, chans, cols = right_feat.shape
    rows = double_rows // 2
    chunks = chunk_count(rows)
    step = rows // chunks
    halves = right_feat.reshape(2, chunks, step, chans, cols)
    raw_mid = [
        from_behind(halves[:, index].reshape(2 * step, chans, cols), "col", 1)
        for index in range(chunks - 1)
    ]
    near = to_rows(right_feat, 0, 1)
    left_feat, valid, grad_out, near = lax.optimization_barrier(
        (left_feat, valid, grad_out, near)
    )
    last_near = near[rows - step :]
    if raw_mid:
        raw_mid, last_near = lax.optimization_barrier((raw_mid, last_near))
    raw_far = [from_behind(part, "col", 1) for part in raw_mid]
    last_mid = from_behind(last_near, "col", 1)
    mid = [to_rows(part, 0, 1) for part in raw_mid] + [last_mid]
    left = to_rows(left_feat, 0, 1)
    keep_cols = valid.astype(F32)
    planes = to_rows(jnp.stack([keep_cols, grad_out * keep_cols]), 1, 2)
    keep, grad_top = planes[0], planes[1]
    far = [to_rows(part, 0, 1) for part in raw_far] + [from_behind(last_mid, "col", 1)]
    windows = [(far_part, mid_part, near) for far_part, mid_part in zip(far, mid)]
    matched = [
        match(offsets, left, index * step, window) for index, window in enumerate(windows)
    ]
    flipped = [stats.T for _, stats in matched]
    mean_level = jnp.concatenate([part[:step] for part in flipped])
    spread = jnp.concatenate([part[LANES // 2 : LANES // 2 + step] for part in flipped])
    coarse = offsets[0].astype(F32) / DISP + mean_level
    fields = jnp.stack([coarse * keep, spread * keep, grad_top])
    fields = with_halo(fields, ("row", "ch"), 1, HALO)
    fields = with_halo(fields, "col", 2, HALO)
    row_at = lax.axis_index(("row", "ch")) * rows - HALO + jnp.arange(rows + 2 * HALO)
    col_at = lax.axis_index("col") * cols - HALO + jnp.arange(cols + 2 * HALO)
    row_in = (row_at >= 0) & (row_at < rows * lax.axis_size(("row", "ch")))
    col_in = (col_at >= 0) & (col_at < cols * lax.axis_size("col"))
    inside = (row_in[:, None] & col_in[None, :]).astype(F32)
    results = refine(jnp.concatenate([fields, inside[None]]), w_first, w_middle, w_last)
    results = results[:, HALO : HALO + rows, HALO : HALO + cols]
    refined = keep * (coarse + results[0])
    gap = jnp.zeros((LANES // 2 - rows, cols), F32)
    cots = jnp.concatenate(
        [grad_top + results[1] * keep, gap, results[2] * keep, gap]
    ).T
    left_parts, right_parts = [], []
    for index, (window, (probs, stats)) in enumerate(zip(windows, matched)):
        grad_left, far_grad, mid_grad, near_grad = match_grads(
            offsets, left, index * step, window, probs, stats, cots
        )
        left_parts.append(grad_left)
        swap = index == chunks - 1
        if swap:
            far_grad, mid_grad, near_grad = (
                to_rows(part, 1, 0) for part in (far_grad, mid_grad, near_grad)
            )
        carried = from_behind(far_grad, "col", -1)
        carried = from_behind((mid_grad + carried.astype(F32)).astype(BF16), "col", -1)
        total = (near_grad + carried.astype(F32)).astype(BF16)
        total = total if swap else to_rows(total, 1, 0)
        right_parts.append(total.reshape(2, step, chans, cols))
    grad_right = jnp.stack(right_parts, axis=1).reshape(double_rows, chans, cols)
    grad_left = to_rows(jnp.concatenate(left_parts), 1, 0)
    return (to_rows(refined, 1, 0), grad_left, grad_right)


def solution(mesh):
    placed = (
        P(("slab", "row"), "ch", "col"),
        P(("slab", "row"), "ch", "col"),
        P(("slab", "col")),
        P(("slab", "row"), ("col", "ch")),
        P(),
        P(),
        P(),
        P(("slab", "row"), ("col", "ch")),
    )
    return jax.shard_map(
        shards,
        mesh=mesh,
        in_specs=placed,
        out_specs=(
            P(("slab", "row"), ("col", "ch")),
            P(("slab", "row"), "ch", "col"),
            P(("slab", "row"), "ch", "col"),
        ),
        check_vma=False,
    )
```

```python
import functools
import math

import jax
import jax.numpy as jnp
from jax import lax
from jax.experimental import pallas as pl
from jax.experimental.pallas import tpu as pltpu
from jax.sharding import PartitionSpec as P

FEAT = 128
DISP = 256
HALO = 4
LANES = 128
CHUNKS = 2
PER_STEP = 4
VMEM = 56 * 1024 * 1024
F32, BF16 = jnp.float32, jnp.bfloat16


def from_behind(value, axis, steps):
    count = lax.axis_size(axis)
    first, last = (max(0, -steps), min(count, count - steps))
    return lax.ppermute(value, axis, [(source, source + steps) for source in range(first, last)])


def with_halo(shard, axis, dim, width):
    length = shard.shape[dim]
    before = from_behind(lax.slice_in_dim(shard, length - width, length, axis=dim), axis, 1)
    after = from_behind(lax.slice_in_dim(shard, 0, width, axis=dim), axis, -1)
    return jnp.concatenate([before, shard, after], axis=dim)


def band_of(offset, window_refs, tile, slot):
    window = jnp.concatenate([ref[slot] for ref in window_refs], axis=1).astype(F32)
    span = window.shape[1]
    start = span - tile - DISP - offset
    return pltpu.roll(window, span - start, 1)[:, : tile + DISP].astype(BF16)


def skew_out(products):
    tile, span = products.shape
    row_ids = lax.broadcasted_iota(jnp.int32, products.shape, 0)
    for bit in (1, 2, 4):
        products = jnp.where((row_ids & bit) != 0, pltpu.roll(products, span - bit, 1), products)
    pieces = [
        pltpu.roll(products[base : base + 8], span - base - 1, 1)[:, :DISP]
        for base in range(0, tile, 8)
    ]
    return jnp.concatenate(pieces, axis=0)


def skew_in(values, span):
    tile = values.shape[0]
    padded = jnp.concatenate([values, jnp.zeros((tile, span - DISP), values.dtype)], axis=1)
    pieces = [pltpu.roll(padded[base : base + 8], base + 1, 1) for base in range(0, tile, 8)]
    skewed = jnp.concatenate(pieces, axis=0)
    row_ids = lax.broadcasted_iota(jnp.int32, skewed.shape, 0)
    for bit in (1, 2, 4):
        skewed = jnp.where((row_ids & bit) != 0, pltpu.roll(skewed, bit, 1), skewed)
    return skewed


def levels_of(shape):
    return (DISP - 1 - lax.broadcasted_iota(jnp.int32, shape, 1)).astype(F32) / DISP


def cost_kernel(offset_ref, left_ref, far_ref, mid_ref, near_ref, probs_ref, stats_ref):
    count, _, tile = left_ref.shape
    lanes = lax.broadcasted_iota(jnp.int32, stats_ref.shape, 1)

    @pl.when(pl.program_id(0) == 0)
    def _():
        stats_ref[...] = jnp.zeros_like(stats_ref)

    stats = stats_ref[...]
    for slot in range(count):
        row = pl.program_id(0) * count + slot
        band = band_of(offset_ref[0], (far_ref, mid_ref, near_ref), tile, slot)
        products = lax.dot_general(
            left_ref[slot], band, (((0,), (0,)), ((), ())), preferred_element_type=F32
        )
        scores = skew_out(products) / math.sqrt(FEAT)
        exps = jnp.exp(scores - jnp.max(scores, axis=1, keepdims=True))
        probs = exps / jnp.sum(exps, axis=1, keepdims=True)
        levels = levels_of(probs.shape)
        mean = jnp.sum(probs * levels, axis=1, keepdims=True)
        spread = jnp.sum(probs * (levels - mean) ** 2, axis=1, keepdims=True)
        probs_ref[slot] = probs
        stats = jnp.where(
            lanes == row, mean, jnp.where(lanes == row + LANES // 2, spread, stats)
        )
    stats_ref[...] = stats


def grad_kernel(
    base, offset_ref, left_ref, far_ref, mid_ref, near_ref, probs_ref, stats_ref, cots_ref,
    left_out, far_out, mid_out, near_out,
):
    count, _, tile = left_ref.shape
    for slot in range(count):
        row = pl.program_id(0) * count + slot
        offset = offset_ref[0]
        band = band_of(offset, (far_ref, mid_ref, near_ref), tile, slot)
        lanes = lax.broadcasted_iota(jnp.int32, stats_ref.shape, 1)

        def column(ref, index):
            return jnp.sum(jnp.where(lanes == index, ref[...], 0.0), axis=1, keepdims=True)

        mean = column(stats_ref, row)
        spread = column(stats_ref, row + LANES // 2)
        cot_mean = column(cots_ref, row + base)
        cot_spread = column(cots_ref, row + base + LANES // 2)
        probs = probs_ref[slot]
        apart = levels_of(probs.shape) - mean
        grad_scores = probs * (cot_mean * apart + cot_spread * (apart * apart - spread))
        grad_cost = (grad_scores / math.sqrt(FEAT)).astype(BF16).astype(F32)
        skewed = skew_in(grad_cost, tile + DISP).astype(BF16)
        left_grad = lax.dot_general(
            band, skewed, (((1,), (1,)), ((), ())), preferred_element_type=F32
        )
        left_out[slot] = left_grad.astype(BF16)
        right_grad = jnp.dot(left_ref[slot], skewed, preferred_element_type=F32)
        span = 3 * tile
        padded = jnp.concatenate(
            [right_grad, jnp.zeros((right_grad.shape[0], span - tile - DISP), F32)], axis=1
        )
        moved = pltpu.roll(padded, span - tile - DISP - offset, 1)
        far_out[slot] = moved[:, :tile].astype(BF16)
        mid_out[slot] = moved[:, tile : 2 * tile]
        near_out[slot] = moved[:, 2 * tile :]


def split_halves(values):
    upper = values.astype(BF16)
    return upper, (values - upper.astype(F32)).astype(BF16)


def weight_side(matrix, rows, depth):
    padded = jnp.pad(matrix, ((0, rows - matrix.shape[0]), (0, depth - matrix.shape[1])))
    upper, lower = split_halves(padded)
    return jnp.concatenate([upper, upper, lower], axis=1)


def field_side(values):
    upper, lower = split_halves(values)
    return jnp.concatenate([upper, lower, upper], axis=0)


def refine_kernel(
    stride, fields_ref, first_ref, middle_ref, last_ref, last_back_ref, middle_back_ref,
    first_back_ref, out_ref, slope_one, slope_two, packed, spread_out,
):
    cells = fields_ref.shape[1]
    chans = slope_one.shape[0]
    taps = [(a - 1) * stride + (b - 1) for a in range(3) for b in range(3)]

    def ahead(values, steps):
        return values if steps == 0 else pltpu.roll(values, -steps % cells, 1)

    def gather(rows, sign, depth):
        parts = [ahead(rows, sign * tap) for tap in taps]
        count = sum(part.shape[0] for part in parts)
        parts.append(jnp.zeros((depth - count, cells), F32))
        return jnp.concatenate(parts, axis=0)

    def product(weights_ref, values):
        return jnp.dot(weights_ref[...], field_side(values), preferred_element_type=F32)

    def scatter(rows_of, sign):
        total = None
        for index, tap in enumerate(taps):
            part = ahead(rows_of(index), sign * tap)
            total = part if total is None else total + part
        return total

    def silu_parts(values):
        sig = 1.0 / (1.0 + jnp.exp(-values))
        return values * sig, sig * (1.0 + values * (1.0 - sig))

    def middle(weights_ref, sign):
        spread_out[...] = jnp.dot(weights_ref[...], packed[...], preferred_element_type=F32)
        return scatter(lambda index: spread_out[index * chans : (index + 1) * chans], sign)

    inside = fields_ref[3:4]
    hidden, slope = silu_parts(product(first_ref, gather(fields_ref[0:2], 1, chans)))
    slope_one[...] = slope * inside
    packed[...] = field_side(hidden * inside)
    hidden, slope = silu_parts(middle(middle_ref, 1))
    slope_two[...] = slope * inside
    rows = product(last_ref, hidden * inside)
    out_ref[0:1] = scatter(lambda index: rows[index : index + 1], 1)
    grad_two = product(last_back_ref, gather(fields_ref[2:3], -1, chans)) * slope_two[...]
    packed[...] = field_side(grad_two)
    grad_one = middle(middle_back_ref, -1) * slope_one[...]
    rows = product(first_back_ref, grad_one)
    out_ref[1:3] = scatter(lambda index: rows[2 * index : 2 * index + 2], -1)
    out_ref[3:8] = jnp.zeros((5, cells), F32)


def refine(fields, w_first, w_middle, w_last):
    count, rows, cols = fields.shape
    cells = rows * cols
    padded_cells = -(-cells // 256) * 256
    flat = jnp.pad(fields.reshape(count, cells), ((0, 8 - count), (0, padded_cells - cells)))
    chans = w_middle.shape[2]
    first = weight_side(w_first.transpose(2, 0, 1, 3).reshape(chans, -1), chans, chans)
    middle = weight_side(w_middle.reshape(-1, chans), 9 * chans, chans)
    last = weight_side(w_last.reshape(9, chans), 16, chans)
    last_back = weight_side(w_last.reshape(9, chans).T, chans, chans)
    middle_back = weight_side(w_middle.transpose(0, 1, 3, 2).reshape(-1, chans), 9 * chans, chans)
    first_back = weight_side(w_first.transpose(0, 1, 3, 2).reshape(-1, chans), chans, chans)
    out = pl.pallas_call(
        functools.partial(refine_kernel, cols),
        out_shape=jax.ShapeDtypeStruct((8, padded_cells), F32),
        in_specs=[pl.BlockSpec(memory_space=pltpu.VMEM)] * 7,
        out_specs=pl.BlockSpec(memory_space=pltpu.VMEM),
        scratch_shapes=[
            pltpu.VMEM((chans, padded_cells), F32),
            pltpu.VMEM((chans, padded_cells), F32),
            pltpu.VMEM((3 * chans, padded_cells), BF16),
            pltpu.VMEM((9 * chans, padded_cells), F32),
        ],
        compiler_params=pltpu.CompilerParams(vmem_limit_bytes=VMEM),
        name="refine",
    )(flat, first, middle, last, last_back, middle_back, first_back)
    return out[:3, :cells].reshape(3, rows, cols)


def per_step(rows):
    return math.gcd(rows, PER_STEP)


def row_block(array, per, base=0):
    return pl.BlockSpec((per,) + array.shape[1:], lambda row: (row + base // per, 0, 0))


def whole_block(shape):
    return pl.BlockSpec(shape, lambda row: (0, 0))


def cost_of(rows, tile):
    return pl.CostEstimate(
        flops=rows * tile * (3 * tile) * FEAT * 2,
        bytes_accessed=rows * tile * DISP * 64,
        transcendentals=rows * tile * DISP,
    )


def match(offsets, left, base, window):
    tile = left.shape[2]
    rows = window[0].shape[0]
    per = per_step(rows)
    probs = jax.ShapeDtypeStruct((rows, tile, DISP), F32)
    stats = jax.ShapeDtypeStruct((tile, LANES), F32)
    return pl.pallas_call(
        cost_kernel,
        grid=(rows // per,),
        in_specs=[pl.BlockSpec(memory_space=pltpu.SMEM), row_block(left, per, base)]
        + [row_block(part, per) for part in window],
        out_specs=[row_block(probs, per), whole_block(stats.shape)],
        out_shape=[probs, stats],
        compiler_params=pltpu.CompilerParams(vmem_limit_bytes=VMEM),
        cost_estimate=cost_of(rows, tile),
        name="match",
    )(offsets, left, *window)


def match_grads(offsets, left, base, window, probs, stats, cots):
    feats, tile = left.shape[1:]
    rows = window[0].shape[0]
    per = per_step(rows)
    narrow = jax.ShapeDtypeStruct((rows, feats, tile), BF16)
    wide = jax.ShapeDtypeStruct((rows, feats, tile), F32)
    return pl.pallas_call(
        functools.partial(grad_kernel, base),
        grid=(rows // per,),
        in_specs=[pl.BlockSpec(memory_space=pltpu.SMEM), row_block(left, per, base)]
        + [row_block(part, per) for part in window]
        + [row_block(probs, per), whole_block(stats.shape), whole_block(cots.shape)],
        out_specs=[row_block(narrow, per)] * 4,
        out_shape=[narrow, narrow, wide, wide],
        compiler_params=pltpu.CompilerParams(vmem_limit_bytes=VMEM),
        cost_estimate=cost_of(rows, tile),
        name="match_grads",
    )(offsets, left, *window, probs, stats, cots)


def to_rows(array, rows_dim, other_dim):
    return lax.all_to_all(array, "ch", rows_dim, other_dim, tiled=True)


def chunk_count(rows):
    return CHUNKS if rows % CHUNKS == 0 else 1


def shards(left_feat, right_feat, offsets, valid, w_first, w_middle, w_last, grad_out):
    whole_near = to_rows(right_feat, 0, 1)
    left_feat, valid, grad_out, whole_near = lax.optimization_barrier(
        (left_feat, valid, grad_out, whole_near)
    )
    rows, _, cols = whole_near.shape
    chunks = chunk_count(rows)
    step = rows // chunks
    near = [whole_near[index * step : (index + 1) * step] for index in range(chunks)]
    mid = []
    for index in range(chunks):
        if mid:
            mid[-1], near[index] = lax.optimization_barrier((mid[-1], near[index]))
        mid.append(from_behind(near[index], "col", 1))
    left = to_rows(left_feat, 0, 1)
    keep_cols = valid.astype(F32)
    planes = to_rows(jnp.stack([keep_cols, grad_out * keep_cols]), 1, 2)
    keep, grad_top = planes[0], planes[1]
    far = [from_behind(part, "col", 1) for part in mid]
    windows = list(zip(far, mid, near))
    matched = [
        match(offsets, left, index * step, window) for index, window in enumerate(windows)
    ]
    flipped = [stats.T for _, stats in matched]
    mean_level = jnp.concatenate([part[:step] for part in flipped])
    spread = jnp.concatenate([part[LANES // 2 : LANES // 2 + step] for part in flipped])
    coarse = offsets[0].astype(F32) / DISP + mean_level
    fields = jnp.stack([coarse * keep, spread * keep, grad_top])
    fields = with_halo(fields, ("row", "ch"), 1, HALO)
    fields = with_halo(fields, "col", 2, HALO)
    row_at = lax.axis_index(("row", "ch")) * rows - HALO + jnp.arange(rows + 2 * HALO)
    col_at = lax.axis_index("col") * cols - HALO + jnp.arange(cols + 2 * HALO)
    row_in = (row_at >= 0) & (row_at < rows * lax.axis_size(("row", "ch")))
    col_in = (col_at >= 0) & (col_at < cols * lax.axis_size("col"))
    inside = (row_in[:, None] & col_in[None, :]).astype(F32)
    results = refine(jnp.concatenate([fields, inside[None]]), w_first, w_middle, w_last)
    results = results[:, HALO : HALO + rows, HALO : HALO + cols]
    refined = keep * (coarse + results[0])
    gap = jnp.zeros((LANES // 2 - rows, cols), F32)
    cots = jnp.concatenate(
        [grad_top + results[1] * keep, gap, results[2] * keep, gap]
    ).T
    left_parts, right_parts = [], []
    for index, (window, (probs, stats)) in enumerate(zip(windows, matched)):
        grad_left, far_grad, mid_grad, near_grad = match_grads(
            offsets, left, index * step, window, probs, stats, cots
        )
        carried = from_behind(far_grad, "col", -1)
        carried = from_behind((mid_grad + carried.astype(F32)).astype(BF16), "col", -1)
        left_parts.append(to_rows(grad_left, 1, 0))
        right_parts.append(to_rows((near_grad + carried.astype(F32)).astype(BF16), 1, 0))

    def assemble(parts):
        parts = [part.reshape((2, step) + part.shape[1:]) for part in parts]
        stacked = jnp.stack(parts, axis=1)
        return stacked.reshape((2 * rows,) + stacked.shape[3:])

    return (to_rows(refined, 1, 0), assemble(left_parts), assemble(right_parts))


def solution(mesh):
    placed = (
        P(("slab", "row"), "ch", "col"),
        P(("slab", "row"), "ch", "col"),
        P(("slab", "col")),
        P(("slab", "row"), ("col", "ch")),
        P(),
        P(),
        P(),
        P(("slab", "row"), ("col", "ch")),
    )
    return jax.shard_map(
        shards,
        mesh=mesh,
        in_specs=placed,
        out_specs=(
            P(("slab", "row"), ("col", "ch")),
            P(("slab", "row"), "ch", "col"),
            P(("slab", "row"), "ch", "col"),
        ),
        check_vma=False,
    )
```
